32 devices in a mesh: slab: 16 (over z, y, x), chan: 2 (over core).
Axes of the slice: x: 2, y: 2, z: 4, core: 2. Of those that a mesh axis runs over, the one named last changes fastest.
Arguments:
- activations: bfloat16 [64, 32, 16, 128], P('chan', 'slab'), may hold values from -6 to 6
- weight: bfloat16 [64, 27, 128], P('chan', None, 'slab'), may hold values from -0.15625 to 0.15625
- cotangent: bfloat16 [128, 32, 16, 128], P('chan', 'slab'), may hold values from -6 to 6
Outputs:
- output: bfloat16 [128, 32, 16, 128], P('chan', 'slab')
- grad_input: bfloat16 [64, 32, 16, 128], P('chan', 'slab')
- grad_weight: float32 [64, 27, 128], P('chan', None, 'slab')
The draws below stay inside these ranges and needn't reach their ends.
All inputs are finite; a program needn't handle non-finite values.
Results may differ from the reference program's by a relative error of at most 0.001.
Values may be sent and summed in bfloat16 or wider, within the bound.
A program may use at most 64 MiB of HBM per device.

```python
import math
import jax
import jax.numpy as jnp
from jax import lax

CIN = 64
COUT = 128
HEIGHT = 16
WIDE = 128
NZ = 32


def spiked(values, stream_key, source, target, shards_of, factor):
    owner, partner = [(jnp.arange(values.shape[dim]) // (values.shape[dim] // shards_of)).reshape([-1 if axis == dim else 1 for axis in range(values.ndim)]) for dim in (source, target)]
    chosen = jax.random.permutation(stream_key, shards_of)[partner]
    strong = (owner == chosen) | (owner == (partner + shards_of // 2) % shards_of)
    return jnp.where(strong, factor * values, values)


def levels(rng, shape, cuts, smallest, top_value):
    gain, own = 1.0, jax.random.fold_in(rng, 6)
    for position, shards_of in cuts:
        heights = jnp.exp(jax.random.uniform(jax.random.fold_in(own, position), (shards_of,), jnp.float32, smallest / len(cuts), top_value / len(cuts)))
        gain = gain * jnp.repeat(heights, shape[position] // shards_of).reshape([-1 if axis == position else 1 for axis in range(len(shape))])
    return gain


def bell_draw(rng, dims, deviation, limit, cuts=(), kind=jnp.bfloat16):
    factor_of = levels(rng, dims, cuts, -0.22, 0.18) if cuts else 1.0
    values = jax.random.normal(rng, dims, jnp.float32) * deviation * factor_of
    return jnp.minimum(jnp.maximum(values, -limit), limit).astype(kind)


def gaussian_with(key, dims, spread, most, cuts, heavy, held_as=jnp.bfloat16):
    entries = spread * jax.random.normal(key, dims, jnp.float32)
    if cuts:
        entries = entries * levels(key, dims, cuts, -0.22, 0.18)
    return jnp.clip(spiked(entries, jax.random.fold_in(key, 3), *heavy), -most, most).astype(held_as)


def setup_inputs(seed: int = 0) -> dict:
    seeds = jax.random.split(jax.random.key(seed), 4)
    return {
        "activations": bell_draw(seeds[0], (CIN, NZ, HEIGHT, WIDE), 1.0, 6.0, ((0, 2), (1, 16))),
        "weight": bell_draw(seeds[1], (CIN, 27, COUT), (27 * CIN) ** -0.5, 0.15625, ((0, 2), (2, 16))),
        "cotangent": gaussian_with(seeds[2], (COUT, NZ, HEIGHT, WIDE), 1.0, 6.0, ((0, 2), (1, 16)), (1, 0, 16, 2.0)),
    }


def to_kernel(weight):
    channels = weight.shape[0]
    outputs = weight.shape[2]
    return weight.reshape(channels, 3, 3, 3, outputs).transpose(1, 2, 3, 0, 4)

def flip_kernel(kernel):
    return kernel[::-1, ::-1, ::-1].transpose(0, 1, 2, 4, 3)

def pad_plane(source):
    return jnp.pad(source, ((0, 0), (0, 0), (1, 1), (1, 1)))

def gather_inputs(source, kernel, depth_out):
    padded = pad_plane(source)
    height = source.shape[2]
    breadth = source.shape[3]
    result = None
    for depth_tap in range(3):
        for row_tap in range(3):
            window = padded[:, depth_tap:depth_tap + depth_out, row_tap:row_tap + height, :]
            stacked = jnp.stack([window[..., col_tap:col_tap + breadth] for col_tap in range(3)])
            addend = jnp.einsum('tczhw,tco->ozhw', stacked.astype(jnp.float32), kernel[depth_tap, row_tap].astype(jnp.float32))
            result = addend if result is None else result + addend
    return result

def filter_terms(source, gradient):
    padded = pad_plane(source)
    depth_out = gradient.shape[1]
    height = source.shape[2]
    breadth = source.shape[3]
    pieces = []
    for depth_tap in range(3):
        for row_tap in range(3):
            window = padded[:, depth_tap:depth_tap + depth_out, row_tap:row_tap + height, :]
            stacked = jnp.stack([window[..., col_tap:col_tap + breadth] for col_tap in range(3)])
            pieces.append(jnp.einsum('tczhw,ozhw->cto', stacked.astype(jnp.float32), gradient.astype(jnp.float32)))
    return jnp.concatenate(pieces, axis=1)

def reference(activations, weight, cotangent):
    kernel = to_kernel(weight)
    flipped = flip_kernel(kernel)
    block_size = math.gcd(NZ, 16)
    block_count = NZ // block_size
    padded_x = jnp.pad(activations, ((0, 0), (1, 1), (0, 0), (0, 0)))
    padded_grad = jnp.pad(cotangent, ((0, 0), (1, 1), (0, 0), (0, 0)))
    starts = jnp.arange(block_count, dtype=jnp.int32) * block_size

    def forward_block(offset):
        source = lax.dynamic_slice_in_dim(padded_x, offset, block_size + 2, 1)
        return gather_inputs(source, kernel, block_size).astype(jnp.bfloat16)

    def backward_block(offset):
        source = lax.dynamic_slice_in_dim(padded_grad, offset, block_size + 2, 1)
        return gather_inputs(source, flipped, block_size).astype(jnp.bfloat16)

    def weight_block(running, offset):
        source = lax.dynamic_slice_in_dim(padded_x, offset, block_size + 2, 1)
        target = lax.dynamic_slice_in_dim(cotangent, offset, block_size, 1)
        return (running + filter_terms(source, target), None)
    output = jnp.moveaxis(lax.map(forward_block, starts), 0, 1).reshape(COUT, NZ, HEIGHT, WIDE)
    grad_input = jnp.moveaxis(lax.map(backward_block, starts), 0, 1).reshape(CIN, NZ, HEIGHT, WIDE)
    grad_weight, _ = lax.scan(weight_block, jnp.zeros((CIN, 27, COUT), jnp.float32), starts)
    grad_scale = 1.0 / math.sqrt(NZ * HEIGHT * WIDE)
    return (output, grad_input, grad_weight * grad_scale)
```

```python
import functools
import math

import jax
import jax.numpy as jnp
from jax import lax
from jax.experimental import pallas as pl
from jax.experimental.pallas import tpu as pltpu
from jax.sharding import PartitionSpec as P

F32 = jnp.float32
BF16 = jnp.bfloat16


def widen(read, write, width, flip):
    lane = None
    rows, full = read.shape
    for h in range(full // width):
        own = read[:, h * width : (h + 1) * width]
        x = own.astype(F32)
        if lane is None:
            lane = lax.broadcasted_iota(jnp.int32, x.shape, 1)
        left = jnp.where(lane == 0, 0.0, pltpu.roll(x, 1, 1)).astype(BF16)
        right = jnp.where(lane == width - 1, 0.0, pltpu.roll(x, width - 1, 1)).astype(BF16)
        first, last = (right, left) if flip else (left, right)
        lanes = slice((h + 1) * width, (h + 2) * width)
        write[0:rows, lanes] = first
        write[rows : 2 * rows, lanes] = own
        write[2 * rows : 3 * rows, lanes] = last


def convolve(kernel_ref, wide_ref, acc_ref, planes, width, flip):
    halo = planes + 2
    outs = acc_ref.shape[1]
    depth = kernel_ref.shape[1]
    full = wide_ref.shape[-1] - 2 * width
    step = min(512, full)
    acc_ref[...] = jnp.zeros_like(acc_ref)
    for zi in range(halo):
        taps = []
        for a in range(3):
            zo = zi + a - 2 if flip else zi - a
            if 0 <= zo < planes:
                taps.append((a, zo))
        low = taps[0][0]
        high = taps[-1][0] + 1

        def chunk(n, carry, zi=zi, taps=taps, low=low, high=high):
            base = pl.multiple_of(n * step, step)
            source = wide_ref[zi, :, :, pl.ds(width + base, step)].reshape(depth, step)
            product = jnp.dot(
                kernel_ref[low * 3 * outs : high * 3 * outs, :], source, preferred_element_type=F32
            )
            for a, zo in taps:
                for b in range(3):
                    shift = b * width if flip else (2 - b) * width
                    lanes = pl.ds(pl.multiple_of(base + shift, width), step)
                    start = ((a - low) * 3 + b) * outs
                    acc_ref[zo, :, lanes] += product[start : start + outs, :]
            return carry

        lax.fori_loop(0, full // step, chunk, 0)


def filter_sums(me, in_ref, grad_ref, gw_ref, planes, width, scale):
    full = in_ref.shape[-1] - 2 * width
    step = min(512, full)
    own = grad_ref.shape[2] // 3
    parts = full // step
    gw_ref[...] = jnp.zeros_like(gw_ref)

    def chunk(n, carry):
        zo = n // parts
        base = pl.multiple_of((n % parts) * step, step)
        left = jnp.concatenate(
            [
                in_ref[zo + a, me, :, pl.ds(pl.multiple_of(base + b * width, width), step)]
                for a in range(3)
                for b in range(3)
            ],
            axis=0,
        )
        right = jnp.concatenate(
            [
                grad_ref[zo + 1, j, own : 2 * own, pl.ds(pl.multiple_of(base + width, width), step)]
                for j in range(2)
            ],
            axis=0,
        )
        gw_ref[...] += lax.dot_general(
            left, right, (((1,), (1,)), ((), ())), preferred_element_type=F32
        )
        return carry

    lax.fori_loop(0, planes * parts, chunk, 0)
    gw_ref[...] = gw_ref[...] * scale


def kernel(planes, width, scale, x_ref, g_ref, wo_ref, wg_ref, out_ref, gi_ref, gw_ref, x3, g3, acc_o, acc_i):
    me = lax.axis_index("chan")
    halo = planes + 2
    full = x_ref.shape[-1]
    for buf in (x3, g3):
        edge = jnp.zeros(buf.shape[:3] + (width,), BF16)
        buf[:, :, :, 0:width] = edge
        buf[:, :, :, width + full : 2 * width + full] = edge
    for zi in range(halo):
        for j in range(2):
            widen(x_ref.at[j, zi], x3.at[zi, j], width, False)
            widen(g_ref.at[j, zi], g3.at[zi, j], width, True)
    filter_sums(me, x3, g3, gw_ref, planes, width, scale)
    convolve(wo_ref, x3, acc_o, planes, width, False)
    convolve(wg_ref, g3, acc_i, planes, width, True)
    out_ref[...] = acc_o[:, :, width : width + full].astype(BF16)
    gi_ref[...] = acc_i[:, :, width : width + full].astype(BF16)


def halo_planes(x):
    peers = lax.axis_size("slab")
    up = [(i, i + 1) for i in range(peers - 1)]
    down = [(i + 1, i) for i in range(peers - 1)]
    planes = x.shape[1]
    before = lax.ppermute(x[:, planes - 1 :], "slab", up)
    after = lax.ppermute(x[:, :1], "slab", down)
    return jnp.concatenate([before, x, after], axis=1)


def body(activations, weight, cotangent):
    cin, planes, height, width = activations.shape
    cout = cotangent.shape[0]
    full = height * width
    me = lax.axis_index("chan")
    x = activations.transpose(1, 0, 2, 3).reshape(planes, cin, full)
    g = cotangent.transpose(1, 0, 2, 3).reshape(planes, cout, full)
    x = lax.all_gather(halo_planes(x[None]), "chan", axis=0, tiled=True)
    g = lax.all_gather(halo_planes(g[None]), "chan", axis=0, tiled=True)
    full_weight = lax.all_gather(weight, "slab", axis=2, tiled=True)
    every_weight = lax.all_gather(full_weight, "chan", axis=0, tiled=True)
    own = lax.dynamic_slice_in_dim(every_weight, me * cout, cout, 2)
    wo = own.reshape(2, cin, 3, 3, 3, cout).transpose(2, 3, 5, 0, 4, 1).reshape(9 * cout, 6 * cin)
    wg = full_weight.reshape(cin, 3, 3, 3, 2, cout).transpose(1, 2, 0, 4, 3, 5).reshape(9 * cin, 6 * cout)
    scale = 1.0 / math.sqrt(planes * lax.axis_size("slab") * full)
    halo = planes + 2
    vmem = pl.BlockSpec(memory_space=pltpu.VMEM)
    output, grad_input, sums = pl.pallas_call(
        functools.partial(kernel, planes, width, scale),
        out_shape=(
            jax.ShapeDtypeStruct((planes, cout, full), BF16),
            jax.ShapeDtypeStruct((planes, cin, full), BF16),
            jax.ShapeDtypeStruct((27 * cin, 2 * cout), F32),
        ),
        in_specs=[vmem] * 4,
        out_specs=(vmem,) * 3,
        scratch_shapes=[
            pltpu.VMEM((halo, 2, 3 * cin, full + 2 * width), BF16),
            pltpu.VMEM((halo, 2, 3 * cout, full + 2 * width), BF16),
            pltpu.VMEM((planes, cout, full + 2 * width), F32),
            pltpu.VMEM((planes, cin, full + 2 * width), F32),
        ],
        compiler_params=pltpu.CompilerParams(vmem_limit_bytes=48 * 1024 * 1024),
    )(x, g, wo, wg)
    output = output.transpose(1, 0, 2).reshape(cout, planes, height, width)
    grad_input = grad_input.transpose(1, 0, 2).reshape(cin, planes, height, width)
    grad_weight = lax.psum_scatter(sums, "slab", scatter_dimension=1, tiled=True)
    grad_weight = grad_weight.reshape(27, cin, weight.shape[2]).transpose(1, 0, 2)
    return (output, grad_input, grad_weight)


def solution(mesh):
    return jax.shard_map(
        body,
        mesh=mesh,
        in_specs=(
            P("chan", "slab", None, None),
            P("chan", None, "slab"),
            P("chan", "slab", None, None),
        ),
        out_specs=(
            P("chan", "slab", None, None),
            P("chan", "slab", None, None),
            P("chan", None, "slab"),
        ),
        check_vma=False,
    )
```

```python
import functools
import math

import jax
import jax.numpy as jnp
from jax import lax
from jax.experimental import pallas as pl
from jax.experimental.pallas import tpu as pltpu
from jax.sharding import PartitionSpec as P

F32 = jnp.float32
BF16 = jnp.bfloat16


def widen(read, write, width, flip):
    lane = None
    rows, full = read.shape
    for h in range(full // width):
        own = read[:, h * width : (h + 1) * width]
        x = own.astype(F32)
        if lane is None:
            lane = lax.broadcasted_iota(jnp.int32, x.shape, 1)
        left = jnp.where(lane == 0, 0.0, pltpu.roll(x, 1, 1)).astype(BF16)
        right = jnp.where(lane == width - 1, 0.0, pltpu.roll(x, width - 1, 1)).astype(BF16)
        first, last = (right, left) if flip else (left, right)
        lanes = slice((h + 1) * width, (h + 2) * width)
        write[0:rows, lanes] = first
        write[rows : 2 * rows, lanes] = own
        write[2 * rows : 3 * rows, lanes] = last


MESH = pl.DeviceIdType.MESH


def send(source, target, send_sem, recv_sem, device):
    return pltpu.make_async_remote_copy(
        src_ref=source,
        dst_ref=target,
        send_sem=send_sem,
        recv_sem=recv_sem,
        device_id=device,
        device_id_type=MESH,
    )


def greet(peers):
    slab = lax.axis_index("slab")
    barrier = pltpu.get_barrier_semaphore()

    def hello(k, carry):
        pl.semaphore_signal(
            barrier, inc=1, device_id={"slab": lax.rem(slab + k, peers)}, device_id_type=MESH
        )
        return carry

    lax.fori_loop(1, peers, hello, 0)
    other = {"chan": 1 - lax.axis_index("chan")}
    pl.semaphore_signal(barrier, inc=1, device_id=other, device_id_type=MESH)
    pl.semaphore_wait(barrier, peers)


def each_peer(peers, action):
    def step(k, carry):
        action(k)
        return carry

    lax.fori_loop(1, peers, step, 0)


def gather_kernel(peers, w_ref, own_ref, other_ref, send_sem, recv_sem, pair_sem):
    slab = lax.axis_index("slab")
    me = lax.axis_index("chan")
    half = peers // 2
    greet(peers)

    def push(k):
        to = lax.rem(slab + k, peers)
        return send(w_ref, own_ref.at[slab], send_sem.at[k], recv_sem.at[slab], {"slab": to})

    def pull(k):
        origin = lax.rem(slab + peers - k, peers)
        return send(w_ref, own_ref.at[origin], send_sem.at[k], recv_sem.at[origin], {"slab": origin})

    each_peer(peers, lambda k: push(k).start())
    own_ref[slab] = w_ref[...]
    each_peer(peers, lambda k: pull(k).wait_recv())
    pair = send(
        own_ref.at[pl.ds((1 - me) * half, half)],
        other_ref,
        pair_sem.at[0],
        pair_sem.at[1],
        {"chan": 1 - me},
    )
    pair.start()
    each_peer(peers, lambda k: push(k).wait_send())
    pair.wait()


def convolve(kernel_ref, wide_ref, acc_ref, planes, width, flip, inputs):
    outs = acc_ref.shape[1]
    depth = kernel_ref.shape[1]
    full = wide_ref.shape[-1] - 2 * width
    step = min(512, full)
    for zi in inputs:
        taps = []
        for a in range(3):
            zo = zi + a - 2 if flip else zi - a
            if 0 <= zo < planes:
                taps.append((a, zo))
        low = taps[0][0]
        high = taps[-1][0] + 1

        def chunk(n, carry, zi=zi, taps=taps, low=low, high=high):
            base = pl.multiple_of(n * step, step)
            source = wide_ref[zi, :, :, pl.ds(width + base, step)].reshape(depth, step)
            product = jnp.dot(
                kernel_ref[low * 3 * outs : high * 3 * outs, :], source, preferred_element_type=F32
            )
            for a, zo in taps:
                for b in range(3):
                    shift = b * width if flip else (2 - b) * width
                    lanes = pl.ds(pl.multiple_of(base + shift, width), step)
                    start = ((a - low) * 3 + b) * outs
                    acc_ref[zo, :, lanes] += product[start : start + outs, :]
            return carry

        lax.fori_loop(0, full // step, chunk, 0)


def filter_sums(me, in_ref, grad_ref, gw_ref, planes, width):
    full = in_ref.shape[-1] - 2 * width
    step = min(512, full)
    own = grad_ref.shape[2] // 3
    parts = full // step
    rows = 9 * in_ref.shape[2]
    gw_ref[...] = jnp.zeros_like(gw_ref)

    def chunk(n, carry):
        zo = n // parts
        base = pl.multiple_of((n % parts) * step, step)
        left = jnp.concatenate(
            [
                in_ref[zo + a, me, :, pl.ds(pl.multiple_of(base + b * width, width), step)]
                for a in range(3)
                for b in range(3)
            ],
            axis=0,
        )
        right = jnp.concatenate(
            [
                grad_ref[zo + 1, j, own : 2 * own, pl.ds(pl.multiple_of(base + width, width), step)]
                for j in range(2)
            ],
            axis=0,
        )
        gw_ref[0:rows, :] += lax.dot_general(
            left, right, (((1,), (1,)), ((), ())), preferred_element_type=F32
        )
        return carry

    lax.fori_loop(0, planes * parts, chunk, 0)


def kernel(
    planes, width, peers, scale,
    x_ref, g_ref, wo_ref, wg_ref, out_ref, gi_ref, sum_ref,
    hx, px, hg, pg, x3, g3, acc_o, acc_i, gw, parts_buf, landed,
    halo_send, halo_recv, fwd_send, fwd_recv, pair_send, pair_recv, sum_send, sum_recv,
):
    slab = lax.axis_index("slab")
    me = lax.axis_index("chan")
    other = {"chan": 1 - me}
    full = x_ref.shape[-1]
    last = planes - 1
    greet(peers)

    below, above = slab > 0, slab < peers - 1
    def halo(ref, buf, kind, side):
        plane, to = (last, slab + 1) if side == 0 else (0, slab - 1)
        return send(
            ref.at[plane], buf.at[me, side],
            halo_send.at[kind, side], halo_recv.at[kind, side], {"slab": to},
        )

    sources = ((x_ref, hx, 0), (g_ref, hg, 1))
    gives, gets = (above, below), (below, above)
    for ref, buf, kind in sources:
        for side in range(2):
            pl.when(gives[side])(lambda r=ref, b=buf, k=kind, s=side: halo(r, b, k, s).start())
    pairs = [
        send(x_ref, px, pair_send.at[0], pair_recv.at[0], other),
        send(g_ref, pg, pair_send.at[1], pair_recv.at[1], other),
    ]
    for pair in pairs:
        pair.start()

    for buf in (x3, g3):
        edge = jnp.zeros(buf.shape[:3] + (width,), BF16)
        buf[:, :, :, 0:width] = edge
        buf[:, :, :, width + full : 2 * width + full] = edge
    acc_o[...] = jnp.zeros_like(acc_o)
    acc_i[...] = jnp.zeros_like(acc_i)
    for z in range(planes):
        widen(x_ref.at[z], x3.at[z + 1, me], width, False)
        widen(g_ref.at[z], g3.at[z + 1, me], width, True)
    for pair in pairs:
        pair.wait_recv()
    for z in range(planes):
        widen(px.at[z], x3.at[z + 1, 1 - me], width, False)
        widen(pg.at[z], g3.at[z + 1, 1 - me], width, True)

    def arrive(ref, buf, wide, kind, flip):
        for side in range(2):
            pl.when(gets[side])(lambda s=side: halo(ref, buf, kind, s).wait_recv())

            @pl.when(jnp.logical_not(gets[side]))
            def _(s=side):
                buf[me, s] = jnp.zeros(buf.shape[2:], BF16)

        forward = send(buf.at[me], buf.at[me], fwd_send.at[kind], fwd_recv.at[kind], other)
        forward.start()
        for side in range(2):
            widen(buf.at[me, side], wide.at[side * (planes + 1), me], width, flip)
        return forward

    def finish(forward, buf, wide, flip):
        forward.wait_recv()
        for side in range(2):
            widen(buf.at[1 - me, side], wide.at[side * (planes + 1), 1 - me], width, flip)

    inner = range(1, planes + 1)
    outer = (0, planes + 1)
    forward_x = arrive(x_ref, hx, x3, 0, False)
    filter_sums(me, x3, g3, gw, planes, width)
    share = parts_buf.shape[1]
    turned = (gw[...] * scale).T
    for s in range(peers):
        parts_buf[s] = turned[s * share : (s + 1) * share, :]

    def push(k):
        to = lax.rem(slab + k, peers)
        return send(
            parts_buf.at[to], landed.at[slab], sum_send.at[k], sum_recv.at[slab], {"slab": to}
        )

    def pull(k):
        origin = lax.rem(slab + peers - k, peers)
        return send(
            parts_buf.at[origin], landed.at[origin], sum_send.at[k], sum_recv.at[origin], {"slab": origin}
        )

    each_peer(peers, lambda k: push(k).start())
    convolve(wo_ref, x3, acc_o, planes, width, False, inner)
    finish(forward_x, hx, x3, False)
    convolve(wo_ref, x3, acc_o, planes, width, False, outer)
    out_ref[...] = acc_o[:, :, width : width + full].astype(BF16)
    convolve(wg_ref, g3, acc_i, planes, width, True, inner)
    forward_g = arrive(g_ref, hg, g3, 1, True)
    finish(forward_g, hg, g3, True)
    convolve(wg_ref, g3, acc_i, planes, width, True, outer)
    gi_ref[...] = acc_i[:, :, width : width + full].astype(BF16)

    landed[slab] = parts_buf[slab]
    each_peer(peers, lambda k: pull(k).wait_recv())
    sum_ref[...] = jnp.sum(landed[...], axis=0)

    each_peer(peers, lambda k: push(k).wait_send())
    for pair in pairs:
        pair.wait_send()
    for forward in (forward_x, forward_g):
        forward.wait_send()
    for ref, buf, kind in sources:
        for side in range(2):
            pl.when(gives[side])(lambda r=ref, b=buf, k=kind, s=side: halo(r, b, k, s).wait_send())


def body(activations, weight, cotangent):
    cin, planes, height, width = activations.shape
    cout = cotangent.shape[0]
    share = weight.shape[2]
    full = height * width
    peers = lax.axis_size("slab")
    half = peers // 2
    me = lax.axis_index("chan")
    vmem = pl.BlockSpec(memory_space=pltpu.VMEM)
    dma = pltpu.SemaphoreType.DMA
    x = activations.transpose(1, 0, 2, 3).reshape(planes, cin, full)
    g = cotangent.transpose(1, 0, 2, 3).reshape(planes, cout, full)

    rows = -(-9 * share // 16) * 16
    lanes = -(-3 * cin // 128) * 128
    shard = weight.reshape(cin, 9, 3, share).transpose(1, 3, 2, 0).reshape(9 * share, 3 * cin)
    shard = jnp.pad(shard, ((0, rows - 9 * share), (0, lanes - 3 * cin)))
    own, theirs = pl.pallas_call(
        functools.partial(gather_kernel, peers),
        out_shape=(
            jax.ShapeDtypeStruct((peers, rows, lanes), BF16),
            jax.ShapeDtypeStruct((half, rows, lanes), BF16),
        ),
        in_specs=[vmem],
        out_specs=(vmem, vmem),
        scratch_shapes=[dma((peers,)), dma((peers,)), dma((2,))],
        compiler_params=pltpu.CompilerParams(
            collective_id=0, has_side_effects=True, vmem_limit_bytes=32 * 1024 * 1024
        ),
    )(shard)
    own = own[:, : 9 * share, : 3 * cin]
    theirs = theirs[:, : 9 * share, : 3 * cin].reshape(half, 9, share, 3 * cin)
    mine = lax.dynamic_slice_in_dim(own, me * half, half, 0).reshape(half, 9, share, 3 * cin)
    pair = [jnp.where(me == 0, mine, theirs), jnp.where(me == 0, theirs, mine)]
    wo = jnp.concatenate(pair, axis=3).transpose(1, 0, 2, 3).reshape(9 * cout, 6 * cin)
    wg = own.reshape(2, half, 9, share, 3, cin).transpose(2, 5, 0, 4, 1, 3).reshape(9 * cin, 6 * cout)

    scale = 1.0 / math.sqrt(planes * peers * full)
    tall = -(-27 * cin // 128) * 128
    padded = full + 2 * width
    output, grad_input, sums = pl.pallas_call(
        functools.partial(kernel, planes, width, peers, scale),
        out_shape=(
            jax.ShapeDtypeStruct((planes, cout, full), BF16),
            jax.ShapeDtypeStruct((planes, cin, full), BF16),
            jax.ShapeDtypeStruct((share, tall), F32),
        ),
        in_specs=[vmem] * 4,
        out_specs=(vmem,) * 3,
        scratch_shapes=[
            pltpu.VMEM((2, 2, cin, full), BF16),
            pltpu.VMEM((planes, cin, full), BF16),
            pltpu.VMEM((2, 2, cout, full), BF16),
            pltpu.VMEM((planes, cout, full), BF16),
            pltpu.VMEM((planes + 2, 2, 3 * cin, padded), BF16),
            pltpu.VMEM((planes + 2, 2, 3 * cout, padded), BF16),
            pltpu.VMEM((planes, cout, padded), F32),
            pltpu.VMEM((planes, cin, padded), F32),
            pltpu.VMEM((tall, 2 * cout), F32),
            pltpu.VMEM((peers, share, tall), F32),
            pltpu.VMEM((peers, share, tall), F32),
            dma((2, 2)), dma((2, 2)), dma((2,)), dma((2,)), dma((2,)), dma((2,)),
            dma((peers,)), dma((peers,)),
        ],
        compiler_params=pltpu.CompilerParams(
            collective_id=1, has_side_effects=True, vmem_limit_bytes=48 * 1024 * 1024
        ),
    )(x, g, wo, wg)
    output = output.transpose(1, 0, 2).reshape(cout, planes, height, width)
    grad_input = grad_input.transpose(1, 0, 2).reshape(cin, planes, height, width)
    grad_weight = sums[:, : 27 * cin].reshape(share, 27, cin).transpose(2, 1, 0)
    return (output, grad_input, grad_weight)


def solution(mesh):
    return jax.shard_map(
        body,
        mesh=mesh,
        in_specs=(
            P("chan", "slab", None, None),
            P("chan", None, "slab"),
            P("chan", "slab", None, None),
        ),
        out_specs=(
            P("chan", "slab", None, None),
            P("chan", "slab", None, None),
            P("chan", None, "slab"),
        ),
        check_vma=False,
    )
```

```python
import functools
import math

import jax
import jax.numpy as jnp
from jax import lax
from jax.experimental import pallas as pl
from jax.experimental.pallas import tpu as pltpu
from jax.sharding import PartitionSpec as P

F32 = jnp.float32
BF16 = jnp.bfloat16


def widen(source, targets, width, flip):
    rows, full = source.shape
    lane = lax.broadcasted_iota(jnp.int32, (rows, width), 1)
    for h in range(full // width):
        own = source[:, h * width : (h + 1) * width]
        x = own.astype(F32)
        left = jnp.where(lane == 0, 0.0, pltpu.roll(x, 1, 1)).astype(BF16)
        right = jnp.where(lane == width - 1, 0.0, pltpu.roll(x, width - 1, 1)).astype(BF16)
        forms = (right, own, left) if flip else (left, own, right)
        lanes = slice((h + 1) * width, (h + 2) * width)
        for target, form in zip(targets, forms):
            target[:, lanes] = form


MESH = pl.DeviceIdType.MESH


def send(source, target, send_sem, recv_sem, device):
    return pltpu.make_async_remote_copy(
        src_ref=source,
        dst_ref=target,
        send_sem=send_sem,
        recv_sem=recv_sem,
        device_id=device,
        device_id_type=MESH,
    )


def greet(peers):
    slab = lax.axis_index("slab")
    barrier = pltpu.get_barrier_semaphore()

    def hello(k, carry):
        pl.semaphore_signal(
            barrier, inc=1, device_id={"slab": lax.rem(slab + k, peers)}, device_id_type=MESH
        )
        return carry

    lax.fori_loop(1, peers, hello, 0)
    other = {"chan": 1 - lax.axis_index("chan")}
    pl.semaphore_signal(barrier, inc=1, device_id=other, device_id_type=MESH)
    pl.semaphore_wait(barrier, peers)


def each_peer(peers, action):
    def step(k, carry):
        action(k)
        return carry

    lax.fori_loop(1, peers, step, 0)


def build_filters(me, share, cin, own_ref, other_ref, stage, wide_o, wo, wg):
    peers = own_ref.shape[0]
    half = peers // 2
    outs = half * share
    for s in range(peers):
        piece = own_ref[s].astype(F32)
        for ab in range(9):
            stage[ab, s * share : (s + 1) * share, :] = piece[ab * share : (ab + 1) * share, :]
    for s in range(half):
        piece = other_ref[s].astype(F32)
        for ab in range(9):
            wide_o[ab * outs + s * share : ab * outs + (s + 1) * share, :] = piece[
                ab * share : (ab + 1) * share, :
            ]
    lanes = wide_o.shape[1]
    wo[:, pl.ds(pl.multiple_of((1 - me) * lanes, lanes), lanes)] = wide_o[...].astype(BF16)
    for ab in range(9):
        block = stage[ab, pl.ds(pl.multiple_of(me * outs, outs), outs), :]
        wo[ab * outs : (ab + 1) * outs, pl.ds(pl.multiple_of(me * lanes, lanes), lanes)] = block.astype(BF16)
        turned = stage[ab].T.astype(BF16)
        for c in range(3):
            wg[ab * cin : (ab + 1) * cin, c * 2 * outs : (c + 1) * 2 * outs] = turned[
                c * cin : (c + 1) * cin, :
            ]


def convolve(kernel_ref, wide_ref, acc_ref, planes, width, flip, inputs):
    outs = acc_ref.shape[1]
    depth = kernel_ref.shape[1]
    middle = (slice(None),) * (wide_ref.ndim - 2)
    full = wide_ref.shape[-1] - 2 * width
    step = min(512, full)
    for zi in inputs:
        taps = []
        for a in range(3):
            zo = zi + a - 2 if flip else zi - a
            if 0 <= zo < planes:
                taps.append((a, zo))
        low = taps[0][0]
        high = taps[-1][0] + 1

        def chunk(n, carry, zi=zi, taps=taps, low=low, high=high):
            base = pl.multiple_of(n * step, step)
            source = wide_ref[(zi,) + middle + (pl.ds(width + base, step),)].reshape(depth, step)
            product = jnp.dot(
                kernel_ref[low * 3 * outs : high * 3 * outs, :], source, preferred_element_type=F32
            )
            for a, zo in taps:
                for b in range(3):
                    shift = b * width if flip else (2 - b) * width
                    lanes = pl.ds(pl.multiple_of(base + shift, width), step)
                    start = ((a - low) * 3 + b) * outs
                    acc_ref[zo, :, lanes] += product[start : start + outs, :]
            return carry

        lax.fori_loop(0, full // step, chunk, 0)


def filter_sums(me, cin, in_ref, grad_ref, gw_ref, planes, width):
    full = in_ref.shape[-1] - 2 * width
    step = min(512, full)
    parts = full // step
    rows = 27 * cin
    gw_ref[...] = jnp.zeros_like(gw_ref)

    def chunk(n, carry):
        zo = n // parts
        base = pl.multiple_of((n % parts) * step, step)
        left = jnp.concatenate(
            [
                in_ref[zo + a, me, 0 : 3 * cin, pl.ds(pl.multiple_of(base + b * width, width), step)]
                for a in range(3)
                for b in range(3)
            ],
            axis=0,
        )
        right = grad_ref[zo + 1, 1, :, :, pl.ds(pl.multiple_of(base + width, width), step)]
        right = right.reshape(gw_ref.shape[1], step)
        gw_ref[0:rows, :] += lax.dot_general(
            left, right, (((1,), (1,)), ((), ())), preferred_element_type=F32
        )
        return carry

    lax.fori_loop(0, planes * parts, chunk, 0)


def kernel(
    planes, width, peers, scale,
    x_ref, g_ref, w_ref, out_ref, gi_ref, sum_ref,
    shards, theirs, stage, wide_o, wo_ref, wg_ref, w_send, w_recv, w_pair, hx, px, hg, pg, x3, g3, acc_o, acc_i, gw, parts_buf, landed,
    halo_send, halo_recv, fwd_send, fwd_recv, pair_send, pair_recv, sum_send, sum_recv,
):
    slab = lax.axis_index("slab")
    me = lax.axis_index("chan")
    other = {"chan": 1 - me}
    full = x_ref.shape[-1]
    last = planes - 1
    cin = x_ref.shape[1]
    half = peers // 2
    greet(peers)

    def into_x(zi, j):
        return [x3.at[zi, j, c * cin : (c + 1) * cin] for c in range(3)]

    def into_g(zi, j):
        return [g3.at[zi, c, j] for c in range(3)]

    def share_out(k):
        to = lax.rem(slab + k, peers)
        return send(w_ref, shards.at[slab], w_send.at[k], w_recv.at[slab], {"slab": to})

    def share_in(k):
        origin = lax.rem(slab + peers - k, peers)
        return send(w_ref, shards.at[origin], w_send.at[k], w_recv.at[origin], {"slab": origin})

    below, above = slab > 0, slab < peers - 1
    def halo(ref, buf, kind, side):
        plane, to = (last, slab + 1) if side == 0 else (0, slab - 1)
        return send(
            ref.at[plane], buf.at[me, side],
            halo_send.at[kind, side], halo_recv.at[kind, side], {"slab": to},
        )

    sources = ((x_ref, hx, 0), (g_ref, hg, 1))
    gives, gets = (above, below), (below, above)
    for ref, buf, kind in sources:
        for side in range(2):
            pl.when(gives[side])(lambda r=ref, b=buf, k=kind, s=side: halo(r, b, k, s).start())
        if kind == 0:
            each_peer(peers, lambda k: share_out(k).start())
    pairs = [
        send(x_ref, px, pair_send.at[0], pair_recv.at[0], other),
        send(g_ref, pg, pair_send.at[1], pair_recv.at[1], other),
    ]
    for pair in pairs:
        pair.start()

    shards[slab] = w_ref[...]
    for lanes in (slice(0, width), slice(width + full, 2 * width + full)):
        x3[:, :, :, lanes] = jnp.zeros(x3.shape[:3] + (width,), BF16)
        g3[:, :, :, :, lanes] = jnp.zeros(g3.shape[:4] + (width,), BF16)
    rest = x3.shape[2] - 3 * cin
    if rest:
        x3[:, :, 3 * cin :, :] = jnp.zeros(x3.shape[:2] + (rest, x3.shape[3]), BF16)
    acc_o[...] = jnp.zeros_like(acc_o)
    acc_i[...] = jnp.zeros_like(acc_i)
    for z in range(planes):
        widen(x_ref.at[z], into_x(z + 1, me), width, False)
        widen(g_ref.at[z], into_g(z + 1, me), width, True)
    for pair in pairs:
        pair.wait_recv()
    for z in range(planes):
        widen(px.at[z], into_x(z + 1, 1 - me), width, False)
        widen(pg.at[z], into_g(z + 1, 1 - me), width, True)

    def arrive(ref, buf, wide, kind, flip):
        for side in range(2):
            pl.when(gets[side])(lambda s=side: halo(ref, buf, kind, s).wait_recv())

            @pl.when(jnp.logical_not(gets[side]))
            def _(s=side):
                buf[me, s] = jnp.zeros(buf.shape[2:], BF16)

        forward = send(buf.at[me], buf.at[me], fwd_send.at[kind], fwd_recv.at[kind], other)
        forward.start()
        for side in range(2):
            widen(buf.at[me, side], wide(side * (planes + 1), me), width, flip)
        return forward

    def finish(forward, buf, wide, flip):
        forward.wait_recv()
        for side in range(2):
            widen(buf.at[1 - me, side], wide(side * (planes + 1), 1 - me), width, flip)

    inner = range(1, planes + 1)
    outer = (0, planes + 1)
    forward_x = arrive(x_ref, hx, into_x, 0, False)
    filter_sums(me, cin, x3, g3, gw, planes, width)
    share = parts_buf.shape[1]
    turned = (gw[...] * scale).T
    for s in range(peers):
        parts_buf[s] = turned[s * share : (s + 1) * share, :]

    def push(k):
        to = lax.rem(slab + k, peers)
        return send(
            parts_buf.at[to], landed.at[slab], sum_send.at[k], sum_recv.at[slab], {"slab": to}
        )

    def pull(k):
        origin = lax.rem(slab + peers - k, peers)
        return send(
            parts_buf.at[origin], landed.at[origin], sum_send.at[k], sum_recv.at[origin], {"slab": origin}
        )

    each_peer(peers, lambda k: push(k).start())
    each_peer(peers, lambda k: share_in(k).wait_recv())
    cross = send(
        shards.at[pl.ds((1 - me) * half, half)], theirs, w_pair.at[0], w_pair.at[1], other
    )
    cross.start()
    cross.wait_recv()
    build_filters(me, parts_buf.shape[1], cin, shards, theirs, stage, wide_o, wo_ref, wg_ref)
    convolve(wo_ref, x3, acc_o, planes, width, False, inner)
    finish(forward_x, hx, into_x, False)
    convolve(wo_ref, x3, acc_o, planes, width, False, outer)
    out_ref[...] = acc_o[:, :, width : width + full].astype(BF16)
    convolve(wg_ref, g3, acc_i, planes, width, True, inner)
    forward_g = arrive(g_ref, hg, into_g, 1, True)
    finish(forward_g, hg, into_g, True)
    convolve(wg_ref, g3, acc_i, planes, width, True, outer)
    gi_ref[...] = acc_i[:, :, width : width + full].astype(BF16)

    landed[slab] = parts_buf[slab]
    each_peer(peers, lambda k: pull(k).wait_recv())
    sum_ref[...] = jnp.sum(landed[...], axis=0)

    each_peer(peers, lambda k: push(k).wait_send())
    for pair in pairs:
        pair.wait_send()
    each_peer(peers, lambda k: share_out(k).wait_send())
    for forward in (forward_x, forward_g, cross):
        forward.wait_send()
    for ref, buf, kind in sources:
        for side in range(2):
            pl.when(gives[side])(lambda r=ref, b=buf, k=kind, s=side: halo(r, b, k, s).wait_send())


def body(activations, weight, cotangent):
    cin, planes, height, width = activations.shape
    cout = cotangent.shape[0]
    share = weight.shape[2]
    full = height * width
    peers = lax.axis_size("slab")
    half = peers // 2
    vmem = pl.BlockSpec(memory_space=pltpu.VMEM)
    dma = pltpu.SemaphoreType.DMA
    x = activations.transpose(1, 0, 2, 3).reshape(planes, cin, full)
    g = cotangent.transpose(1, 0, 2, 3).reshape(planes, cout, full)

    rows = -(-9 * share // 16) * 16
    lanes = -(-3 * cin // 128) * 128
    shard = weight.reshape(cin, 9, 3, share).transpose(1, 3, 2, 0).reshape(9 * share, 3 * cin)
    shard = jnp.pad(shard, ((0, rows - 9 * share), (0, lanes - 3 * cin)))

    scale = 1.0 / math.sqrt(planes * peers * full)
    tall = -(-27 * cin // 128) * 128
    padded = full + 2 * width
    output, grad_input, sums = pl.pallas_call(
        functools.partial(kernel, planes, width, peers, scale),
        out_shape=(
            jax.ShapeDtypeStruct((planes, cout, full), BF16),
            jax.ShapeDtypeStruct((planes, cin, full), BF16),
            jax.ShapeDtypeStruct((share, tall), F32),
        ),
        in_specs=[vmem] * 3,
        out_specs=(vmem,) * 3,
        scratch_shapes=[
            pltpu.VMEM((peers, rows, lanes), BF16),
            pltpu.VMEM((half, rows, lanes), BF16),
            pltpu.VMEM((9, 2 * cout, lanes), F32),
            pltpu.VMEM((9 * cout, lanes), F32),
            pltpu.VMEM((9 * cout, 2 * lanes), BF16),
            pltpu.VMEM((9 * cin, 6 * cout), BF16),
            dma((peers,)), dma((peers,)), dma((2,)),
            pltpu.VMEM((2, 2, cin, full), BF16),
            pltpu.VMEM((planes, cin, full), BF16),
            pltpu.VMEM((2, 2, cout, full), BF16),
            pltpu.VMEM((planes, cout, full), BF16),
            pltpu.VMEM((planes + 2, 2, lanes, padded), BF16),
            pltpu.VMEM((planes + 2, 3, 2, cout, padded), BF16),
            pltpu.VMEM((planes, cout, padded), F32),
            pltpu.VMEM((planes, cin, padded), F32),
            pltpu.VMEM((tall, 2 * cout), F32),
            pltpu.VMEM((peers, share, tall), F32),
            pltpu.VMEM((peers, share, tall), F32),
            dma((2, 2)), dma((2, 2)), dma((2,)), dma((2,)), dma((2,)), dma((2,)),
            dma((peers,)), dma((peers,)),
        ],
        compiler_params=pltpu.CompilerParams(
            collective_id=0, has_side_effects=True, vmem_limit_bytes=48 * 1024 * 1024
        ),
    )(x, g, shard)
    output = output.transpose(1, 0, 2).reshape(cout, planes, height, width)
    grad_input = grad_input.transpose(1, 0, 2).reshape(cin, planes, height, width)
    grad_weight = sums[:, : 27 * cin].reshape(share, 27, cin).transpose(2, 1, 0)
    return (output, grad_input, grad_weight)


def solution(mesh):
    return jax.shard_map(
        body,
        mesh=mesh,
        in_specs=(
            P("chan", "slab", None, None),
            P("chan", None, "slab"),
            P("chan", "slab", None, None),
        ),
        out_specs=(
            P("chan", "slab", None, None),
            P("chan", "slab", None, None),
            P("chan", None, "slab"),
        ),
        check_vma=False,
    )
```

```python
import functools
import math

import jax
import jax.numpy as jnp
from jax import lax
from jax.experimental import pallas as pl
from jax.experimental.pallas import tpu as pltpu
from jax.sharding import PartitionSpec as P

F32 = jnp.float32
BF16 = jnp.bfloat16


def widen(source, rows_ref, targets, flip):
    channels, height, width = source.shape
    lane = lax.broadcasted_iota(jnp.int32, (channels, width), 1)
    rows_ref[0 : channels * height, :] = source[...].astype(F32).reshape(channels * height, width)
    for h in range(height):
        x = rows_ref[pl.ds(h, channels, stride=height), :]
        own = x.astype(BF16)
        left = jnp.where(lane == 0, 0.0, pltpu.roll(x, 1, 1)).astype(BF16)
        right = jnp.where(lane == width - 1, 0.0, pltpu.roll(x, width - 1, 1)).astype(BF16)
        forms = (right, own, left) if flip else (left, own, right)
        lanes = slice((h + 1) * width, (h + 2) * width)
        for target, form in zip(targets, forms):
            target[:, lanes] = form


MESH = pl.DeviceIdType.MESH


def send(source, target, send_sem, recv_sem, device):
    return pltpu.make_async_remote_copy(
        src_ref=source,
        dst_ref=target,
        send_sem=send_sem,
        recv_sem=recv_sem,
        device_id=device,
        device_id_type=MESH,
    )


def greet(peers):
    slab = lax.axis_index("slab")
    barrier = pltpu.get_barrier_semaphore()

    def hello(k, carry):
        pl.semaphore_signal(
            barrier, inc=1, device_id={"slab": lax.rem(slab + k, peers)}, device_id_type=MESH
        )
        return carry

    lax.fori_loop(1, peers, hello, 0)
    other = {"chan": 1 - lax.axis_index("chan")}
    pl.semaphore_signal(barrier, inc=1, device_id=other, device_id_type=MESH)
    pl.semaphore_wait(barrier, peers)


def each_peer(peers, action):
    def step(k, carry):
        action(k)
        return carry

    lax.fori_loop(1, peers, step, 0)


def build_filters(me, share, cin, own_ref, other_ref, stage, wide_o, wo, wg):
    peers = own_ref.shape[0]
    half = peers // 2
    outs = half * share
    for s in range(peers):
        piece = own_ref[s].astype(F32)
        for ab in range(9):
            stage[ab, s * share : (s + 1) * share, :] = piece[ab * share : (ab + 1) * share, :]
    for s in range(half):
        piece = other_ref[s].astype(F32)
        for ab in range(9):
            wide_o[ab * outs + s * share : ab * outs + (s + 1) * share, :] = piece[
                ab * share : (ab + 1) * share, :
            ]
    lanes = wide_o.shape[1]
    wo[:, pl.ds(pl.multiple_of((1 - me) * lanes, lanes), lanes)] = wide_o[...].astype(BF16)
    for ab in range(9):
        block = stage[ab, pl.ds(pl.multiple_of(me * outs, outs), outs), :]
        wo[ab * outs : (ab + 1) * outs, pl.ds(pl.multiple_of(me * lanes, lanes), lanes)] = block.astype(BF16)
        turned = stage[ab].T.astype(BF16)
        for c in range(3):
            wg[ab * cin : (ab + 1) * cin, c * 2 * outs : (c + 1) * 2 * outs] = turned[
                c * cin : (c + 1) * cin, :
            ]


def convolve(kernel_ref, wide_ref, acc_ref, planes, width, flip, inputs):
    outs = acc_ref.shape[1]
    depth = kernel_ref.shape[1]
    middle = (slice(None),) * (wide_ref.ndim - 2)
    full = wide_ref.shape[-1] - 2 * width
    step = min(512, full)
    for zi in inputs:
        taps = []
        for a in range(3):
            zo = zi + a - 2 if flip else zi - a
            if 0 <= zo < planes:
                taps.append((a, zo))
        low = taps[0][0]
        high = taps[-1][0] + 1

        def chunk(n, carry, zi=zi, taps=taps, low=low, high=high):
            base = pl.multiple_of(n * step, step)
            source = wide_ref[(zi,) + middle + (pl.ds(width + base, step),)].reshape(depth, step)
            product = jnp.dot(
                kernel_ref[low * 3 * outs : high * 3 * outs, :], source, preferred_element_type=F32
            )
            for a, zo in taps:
                for b in range(3):
                    shift = b * width if flip else (2 - b) * width
                    lanes = pl.ds(pl.multiple_of(base + shift, width), step)
                    start = ((a - low) * 3 + b) * outs
                    acc_ref[zo, :, lanes] += product[start : start + outs, :]
            return carry

        lax.fori_loop(0, full // step, chunk, 0)


def filter_sums(me, cin, in_ref, grad_ref, gw_ref, planes, width):
    full = in_ref.shape[-1] - 2 * width
    step = min(512, full)
    parts = full // step
    rows = 27 * cin
    gw_ref[...] = jnp.zeros_like(gw_ref)

    def chunk(n, carry):
        zo = n // parts
        base = pl.multiple_of((n % parts) * step, step)
        left = jnp.concatenate(
            [
                in_ref[zo + a, me, 0 : 3 * cin, pl.ds(pl.multiple_of(base + b * width, width), step)]
                for a in range(3)
                for b in range(3)
            ],
            axis=0,
        )
        right = grad_ref[zo + 1, 1, :, :, pl.ds(pl.multiple_of(base + width, width), step)]
        right = right.reshape(gw_ref.shape[1], step)
        gw_ref[0:rows, :] += lax.dot_general(
            left, right, (((1,), (1,)), ((), ())), preferred_element_type=F32
        )
        return carry

    lax.fori_loop(0, planes * parts, chunk, 0)


def kernel(
    planes, width, peers, scale,
    x_ref, g_ref, w_ref, out_ref, gi_ref, sum_ref,
    shards, theirs, stage, wide_o, wo_ref, wg_ref, w_send, w_recv, w_pair, lx, lg, local_sem, rows_x, rows_g, hx, px, hg, pg, x3, g3, acc_o, acc_i, gw, parts_buf, landed,
    halo_send, halo_recv, fwd_send, fwd_recv, pair_send, pair_recv, sum_send, sum_recv,
):
    slab = lax.axis_index("slab")
    me = lax.axis_index("chan")
    other = {"chan": 1 - me}
    full = x_ref.shape[2] * width
    last = planes - 1
    cin = x_ref.shape[0]
    half = peers // 2
    greet(peers)

    def into_x(zi, j):
        return [x3.at[zi, j, c * cin : (c + 1) * cin] for c in range(3)]

    def into_g(zi, j):
        return [g3.at[zi, c, j] for c in range(3)]

    def share_out(k):
        to = lax.rem(slab + k, peers)
        return send(w_ref, shards.at[slab], w_send.at[k], w_recv.at[slab], {"slab": to})

    def share_in(k):
        origin = lax.rem(slab + peers - k, peers)
        return send(w_ref, shards.at[origin], w_send.at[k], w_recv.at[origin], {"slab": origin})

    below, above = slab > 0, slab < peers - 1
    def halo(ref, buf, kind, side):
        plane, to = (last, slab + 1) if side == 0 else (0, slab - 1)
        return send(
            ref.at[:, plane], buf.at[me, side],
            halo_send.at[kind, side], halo_recv.at[kind, side], {"slab": to},
        )

    sources = ((x_ref, hx, 0), (g_ref, hg, 1))
    gives, gets = (above, below), (below, above)
    for ref, buf, kind in sources:
        for side in range(2):
            pl.when(gives[side])(lambda r=ref, b=buf, k=kind, s=side: halo(r, b, k, s).start())
        if kind == 0:
            each_peer(peers, lambda k: share_out(k).start())
    pairs = [
        send(x_ref, px, pair_send.at[0], pair_recv.at[0], other),
        send(g_ref, pg, pair_send.at[1], pair_recv.at[1], other),
    ]
    for pair in pairs:
        pair.start()

    shards[slab] = w_ref[...]
    held = [
        pltpu.make_async_copy(x_ref, lx, local_sem.at[0]),
        pltpu.make_async_copy(g_ref, lg, local_sem.at[1]),
    ]
    for copy in held:
        copy.start()
    for lanes in (slice(0, width), slice(width + full, 2 * width + full)):
        x3[:, :, :, lanes] = jnp.zeros(x3.shape[:3] + (width,), BF16)
        g3[:, :, :, :, lanes] = jnp.zeros(g3.shape[:4] + (width,), BF16)
    rest = x3.shape[2] - 3 * cin
    if rest:
        x3[:, :, 3 * cin :, :] = jnp.zeros(x3.shape[:2] + (rest, x3.shape[3]), BF16)
    acc_o[...] = jnp.zeros_like(acc_o)
    acc_i[...] = jnp.zeros_like(acc_i)
    for copy in held:
        copy.wait()
    for z in range(planes):
        widen(lx.at[:, z], rows_x, into_x(z + 1, me), False)
        widen(lg.at[:, z], rows_g, into_g(z + 1, me), True)
    for pair in pairs:
        pair.wait_recv()
    for z in range(planes):
        widen(px.at[:, z], rows_x, into_x(z + 1, 1 - me), False)
        widen(pg.at[:, z], rows_g, into_g(z + 1, 1 - me), True)

    def arrive(ref, buf, rows, wide, kind, flip):
        for side in range(2):
            pl.when(gets[side])(lambda s=side: halo(ref, buf, kind, s).wait_recv())

            @pl.when(jnp.logical_not(gets[side]))
            def _(s=side):
                buf[me, s] = jnp.zeros(buf.shape[2:], BF16)

        forward = send(buf.at[me], buf.at[me], fwd_send.at[kind], fwd_recv.at[kind], other)
        forward.start()
        for side in range(2):
            widen(buf.at[me, side], rows, wide(side * (planes + 1), me), flip)
        return forward

    def finish(forward, buf, rows, wide, flip):
        forward.wait_recv()
        for side in range(2):
            widen(buf.at[1 - me, side], rows, wide(side * (planes + 1), 1 - me), flip)

    inner = range(1, planes + 1)
    outer = (0, planes + 1)
    forward_x = arrive(x_ref, hx, rows_x, into_x, 0, False)
    filter_sums(me, cin, x3, g3, gw, planes, width)
    share = parts_buf.shape[1]
    turned = (gw[...] * scale).T
    for s in range(peers):
        parts_buf[s] = turned[s * share : (s + 1) * share, :]

    def push(k):
        to = lax.rem(slab + k, peers)
        return send(
            parts_buf.at[to], landed.at[slab], sum_send.at[k], sum_recv.at[slab], {"slab": to}
        )

    def pull(k):
        origin = lax.rem(slab + peers - k, peers)
        return send(
            parts_buf.at[origin], landed.at[origin], sum_send.at[k], sum_recv.at[origin], {"slab": origin}
        )

    each_peer(peers, lambda k: push(k).start())
    each_peer(peers, lambda k: share_in(k).wait_recv())
    cross = send(
        shards.at[pl.ds((1 - me) * half, half)], theirs, w_pair.at[0], w_pair.at[1], other
    )
    cross.start()
    cross.wait_recv()
    build_filters(me, parts_buf.shape[1], cin, shards, theirs, stage, wide_o, wo_ref, wg_ref)
    convolve(wo_ref, x3, acc_o, planes, width, False, inner)
    finish(forward_x, hx, rows_x, into_x, False)
    convolve(wo_ref, x3, acc_o, planes, width, False, outer)
    out_ref[...] = acc_o[:, :, width : width + full].astype(BF16)
    convolve(wg_ref, g3, acc_i, planes, width, True, inner)
    forward_g = arrive(g_ref, hg, rows_g, into_g, 1, True)
    finish(forward_g, hg, rows_g, into_g, True)
    convolve(wg_ref, g3, acc_i, planes, width, True, outer)
    gi_ref[...] = acc_i[:, :, width : width + full].astype(BF16)

    landed[slab] = parts_buf[slab]
    each_peer(peers, lambda k: pull(k).wait_recv())
    sum_ref[...] = jnp.sum(landed[...], axis=0)

    each_peer(peers, lambda k: push(k).wait_send())
    for pair in pairs:
        pair.wait_send()
    each_peer(peers, lambda k: share_out(k).wait_send())
    for forward in (forward_x, forward_g, cross):
        forward.wait_send()
    for ref, buf, kind in sources:
        for side in range(2):
            pl.when(gives[side])(lambda r=ref, b=buf, k=kind, s=side: halo(r, b, k, s).wait_send())


def body(activations, weight, cotangent):
    cin, planes, height, width = activations.shape
    cout = cotangent.shape[0]
    share = weight.shape[2]
    full = height * width
    peers = lax.axis_size("slab")
    half = peers // 2
    vmem = pl.BlockSpec(memory_space=pltpu.VMEM)
    dma = pltpu.SemaphoreType.DMA
    rows = -(-9 * share // 16) * 16
    lanes = -(-3 * cin // 128) * 128
    shard = weight.reshape(cin, 9, 3, share).transpose(1, 3, 2, 0).reshape(9 * share, 3 * cin)
    shard = jnp.pad(shard, ((0, rows - 9 * share), (0, lanes - 3 * cin)))

    scale = 1.0 / math.sqrt(planes * peers * full)
    tall = -(-27 * cin // 128) * 128
    padded = full + 2 * width
    output, grad_input, sums = pl.pallas_call(
        functools.partial(kernel, planes, width, peers, scale),
        out_shape=(
            jax.ShapeDtypeStruct((planes, cout, full), BF16),
            jax.ShapeDtypeStruct((planes, cin, full), BF16),
            jax.ShapeDtypeStruct((share, tall), F32),
        ),
        in_specs=[pl.BlockSpec(memory_space=pl.ANY)] * 2 + [vmem],
        out_specs=(vmem,) * 3,
        scratch_shapes=[
            pltpu.VMEM((peers, rows, lanes), BF16),
            pltpu.VMEM((half, rows, lanes), BF16),
            pltpu.VMEM((9, 2 * cout, lanes), F32),
            pltpu.VMEM((9 * cout, lanes), F32),
            pltpu.VMEM((9 * cout, 2 * lanes), BF16),
            pltpu.VMEM((9 * cin, 6 * cout), BF16),
            dma((peers,)), dma((peers,)), dma((2,)),
            pltpu.VMEM((cin, planes, height, width), BF16),
            pltpu.VMEM((cout, planes, height, width), BF16),
            dma((2,)),
            pltpu.VMEM((cin * height, width), F32),
            pltpu.VMEM((cout * height, width), F32),
            pltpu.VMEM((2, 2, cin, height, width), BF16),
            pltpu.VMEM((cin, planes, height, width), BF16),
            pltpu.VMEM((2, 2, cout, height, width), BF16),
            pltpu.VMEM((cout, planes, height, width), BF16),
            pltpu.VMEM((planes + 2, 2, lanes, padded), BF16),
            pltpu.VMEM((planes + 2, 3, 2, cout, padded), BF16),
            pltpu.VMEM((planes, cout, padded), F32),
            pltpu.VMEM((planes, cin, padded), F32),
            pltpu.VMEM((tall, 2 * cout), F32),
            pltpu.VMEM((peers, share, tall), F32),
            pltpu.VMEM((peers, share, tall), F32),
            dma((2, 2)), dma((2, 2)), dma((2,)), dma((2,)), dma((2,)), dma((2,)),
            dma((peers,)), dma((peers,)),
        ],
        compiler_params=pltpu.CompilerParams(
            collective_id=0, has_side_effects=True, vmem_limit_bytes=48 * 1024 * 1024
        ),
    )(activations, cotangent, shard)
    output = output.transpose(1, 0, 2).reshape(cout, planes, height, width)
    grad_input = grad_input.transpose(1, 0, 2).reshape(cin, planes, height, width)
    grad_weight = sums[:, : 27 * cin].reshape(share, 27, cin).transpose(2, 1, 0)
    return (output, grad_input, grad_weight)


def solution(mesh):
    return jax.shard_map(
        body,
        mesh=mesh,
        in_specs=(
            P("chan", "slab", None, None),
            P("chan", None, "slab"),
            P("chan", "slab", None, None),
        ),
        out_specs=(
            P("chan", "slab", None, None),
            P("chan", "slab", None, None),
            P("chan", None, "slab"),
        ),
        check_vma=False,
    )
```
